256 devices in a mesh: row: 16 (over x, z_lo, core), col: 16 (over z_hi, y).
Axes of the slice: x: 4, y: 4, z: 8 (z_hi: 4, z_lo: 2; z = z_hi * 2 + z_lo), core: 2. Of those that a mesh axis runs over, the one named last changes fastest.
Arguments:
- pre_act: bfloat16 [2048, 24576], P('row', 'col'), may hold values from -6 to 6
- out_grad: bfloat16 [2048, 12288], P('col', 'row'), may hold values from -4 to 4
- down_weight: bfloat16 [24576, 12288], P('col', 'row'), may hold values from -0.0546875 to 0.0546875
Outputs:
- pre_grad: bfloat16 [2048, 24576], P('row', 'col')
- weight_grad: float32 [24576, 12288], P('col', 'row')
The draws below stay inside these ranges and needn't reach their ends.
All inputs are finite; a program needn't handle non-finite values.
Results may differ from the reference program's by a relative error of at most 0.0031.
Values may be sent and summed in bfloat16 or wider, within the bound.
No kernel may reach another device: no remote copies, remote signals or barrier semaphores. Data moves between devices by JAX's collectives and lax.ppermute only.
A program may use at most 128 MiB of HBM per device.

```python
import jax
import jax.numpy as jnp
from jax import lax

D = 12288
F = 24576
TOKENS = 2048


def raised(values, stream_key, source, target, parts, factor):
    def block_of(position):
        return (jnp.arange(values.shape[position]) // (values.shape[position] // parts)).reshape((-1,) + (1,) * (values.ndim - 1 - position))

    one_side = jax.random.permutation(stream_key, parts)[block_of(target)]
    far = (block_of(target) + parts // 2) % parts
    return jnp.where((block_of(source) == one_side) | (block_of(source) == far), factor * values, values)


def steps_of(rng, shape, split, low, largest):
    level = 1.0
    for position, shards_of in split:
        heights = jax.random.uniform(jax.random.fold_in(jax.random.fold_in(rng, 6), position), (shards_of,), jnp.float32, low / len(split), largest / len(split))
        level = level * jnp.repeat(jnp.exp(heights), shape[position] // shards_of).reshape((-1,) + (1,) * (len(shape) - 1 - position))
    return level


def bell_draw(stream_key, shape, deviation, reach, shards=(), dtype=jnp.bfloat16):
    factor_of = steps_of(stream_key, shape, shards, -0.22, 0.18) if shards else 1.0
    entries = jax.random.normal(stream_key, shape, jnp.float32) * deviation * factor_of
    return jnp.minimum(jnp.maximum(entries, -reach), reach).astype(dtype)


def bell_draw_with(own_key, extent, spread, most, cuts, heavy, dtype=jnp.bfloat16):
    result = spread * jax.random.normal(own_key, extent, jnp.float32)
    if cuts:
        result = result * steps_of(own_key, extent, cuts, -0.22, 0.18)
    return jnp.clip(raised(result, jax.random.fold_in(own_key, 3), *heavy), -most, most).astype(dtype)


def setup_inputs(seed: int = 0) -> dict:
    keys = jax.random.split(jax.random.key(seed), 4)
    return {
        "pre_act": bell_draw(keys[0], (TOKENS, F), 1.0, 6.0, ((0, 16), (1, 16))),
        "out_grad": bell_draw_with(keys[1], (TOKENS, D), 0.5, 4.0, ((0, 16), (1, 16)), (1, 0, 16, 2.0)),
        "down_weight": bell_draw(keys[2], (F, D), D ** -0.5, 0.0546875, ((0, 16), (1, 16))),
    }


coeff_k = 0.7978845608
coeff_c = 0.044715


def gelu_value(z):
    t = jnp.tanh(coeff_k * (z + coeff_c * z * z * z))
    return 0.5 * z * (1.0 + t)


def gelu_slope(z):
    t = jnp.tanh(coeff_k * (z + coeff_c * z * z * z))
    return 0.5 * (1.0 + t) + 0.5 * z * (1.0 - t * t) * coeff_k * (1.0 + 3.0 * coeff_c * z * z)


def reference(pre_act, out_grad, down_weight):
    pre_float = pre_act.astype(jnp.float32)
    act = gelu_value(pre_float).astype(jnp.bfloat16)
    hidden_grad = lax.dot_general(out_grad, down_weight, (((1,), (1,)), ((), ())), preferred_element_type=jnp.float32)
    pre_grad = (hidden_grad * gelu_slope(pre_float)).astype(jnp.bfloat16)
    weight_grad = lax.dot_general(act, out_grad, (((0,), (0,)), ((), ())), preferred_element_type=jnp.float32)
    return pre_grad, weight_grad
```

```python
import jax
import jax.numpy as jnp
import numpy as np
from jax import lax
from jax.experimental import pallas as pl
from jax.experimental.pallas import tpu as pltpu
from jax.sharding import Mesh, PartitionSpec as P

coeff_k = 0.7978845608
coeff_c = 0.044715

AXES = ("x", "zl", "core", "zh", "y")
SIZES = {"x": 4, "zl": 2, "core": 2, "zh": 4, "y": 4}
TB = 128
MIB = 1024 * 1024
STEPS = ((2, 1), (1, 0), (3, 0), (1, 1), (3, 1), (0, 1), (2, 0), (0, 0))
KEPT = ((0, 0), (2, 0))
WHOLE = pl.BlockSpec(memory_space=pltpu.VMEM)


def fetch(value, axis, ahead):
    n = SIZES[axis]
    return lax.ppermute(value, axis, [((i + ahead) % n, i) for i in range(n)])


def gather_x(copies):
    return lax.all_to_all(copies, "x", 0, 0).reshape(4 * TB, copies.shape[-1])


def send_xz(value, dx, dz):
    pairs = []
    for x in range(4):
        for z in range(2):
            pairs.append((x * 2 + z, (x + dx) % 4 * 2 + (z + dz) % 2))
    return lax.ppermute(value, ("x", "zl"), pairs)


def tanh_of(z):
    return jnp.tanh(coeff_k * (z + coeff_c * z * z * z))


def gelu_kernel(pre_ref, act_ref):
    z = pre_ref[...].astype(jnp.float32)
    act = (0.5 * z * (1.0 + tanh_of(z))).astype(act_ref.dtype)
    for n in range(act_ref.shape[0]):
        act_ref[n] = act


def slope_kernel(pre_ref, slope_ref):
    z = pre_ref[...].astype(jnp.float32)
    t = tanh_of(z)
    slope_ref[...] = 0.5 * (1.0 + t) + 0.5 * z * (1.0 - t * t) * coeff_k * (1.0 + 3.0 * coeff_c * z * z)


def elementwise(kernel, pre_act, dtype, name, copies=None):
    rows, f = pre_act.shape
    tile = 64
    spec = pl.BlockSpec((tile, f), lambda i: (i, 0))
    many = pl.BlockSpec((copies, tile, f), lambda i: (0, i, 0))
    return pl.pallas_call(
        kernel,
        out_shape=jax.ShapeDtypeStruct((copies, rows, f) if copies else (rows, f), dtype),
        grid=(rows // tile,),
        in_specs=[spec],
        out_specs=many if copies else spec,
        compiler_params=pltpu.CompilerParams(vmem_limit_bytes=8 * MIB),
        name=name,
    )(pre_act)


def order_kernel(idx_ref, *refs):
    sources, (own_ref, other_ref) = refs[:-2], refs[-2:]
    n = 0
    for source in sources:
        for b in range(source.shape[0] // TB):
            place = idx_ref[n]
            rows = pl.ds(pl.multiple_of(place % 8 * TB, TB), TB)

            @pl.when(place < 8)
            def _(source=source, b=b, rows=rows):
                own_ref[rows, :] = source[b * TB : (b + 1) * TB, :]

            @pl.when(place >= 8)
            def _(source=source, b=b, rows=rows):
                other_ref[rows, :] = source[b * TB : (b + 1) * TB, :]

            n += 1


def order(index, sources):
    width = sources[0].shape[1]
    out = jax.ShapeDtypeStruct((8 * TB, width), sources[0].dtype)
    return pl.pallas_call(
        order_kernel,
        out_shape=(out, out),
        in_specs=[pl.BlockSpec(memory_space=pltpu.SMEM)] + [WHOLE] * len(sources),
        out_specs=(WHOLE, WHOLE),
        compiler_params=pltpu.CompilerParams(vmem_limit_bytes=16 * MIB),
        name="order_tokens",
    )(index, *sources)


def terms_kernel(own_ref, other_ref, w_own_ref, w_other_ref, *out_refs):
    dims = (((1,), (1,)), ((), ()))
    for n in range(0, len(out_refs), 2):
        rows = slice(n * TB, (n + 2) * TB)
        acc = lax.dot_general(own_ref[rows, :], w_own_ref[...], dims, preferred_element_type=jnp.float32)
        acc += lax.dot_general(other_ref[rows, :], w_other_ref[...], dims, preferred_element_type=jnp.float32)
        out_refs[n][...] = acc[:TB].astype(out_refs[n].dtype)
        out_refs[n + 1][...] = acc[TB:].astype(out_refs[n + 1].dtype)


def terms(own, other, w_own, w_other):
    f, d = w_own.shape
    rows = own.shape[0]
    tile = 512
    grad_spec = pl.BlockSpec((rows, d), lambda i: (0, 0))
    w_spec = pl.BlockSpec((tile, d), lambda i: (i, 0))
    return pl.pallas_call(
        terms_kernel,
        out_shape=[jax.ShapeDtypeStruct((TB, f), jnp.float32 if k in KEPT else jnp.bfloat16) for k in STEPS],
        grid=(f // tile,),
        in_specs=[grad_spec, grad_spec, w_spec, w_spec],
        out_specs=[pl.BlockSpec((TB, tile), lambda i: (0, i))] * len(STEPS),
        compiler_params=pltpu.CompilerParams(vmem_limit_bytes=24 * MIB),
        cost_estimate=pl.CostEstimate(
            flops=4 * rows * f * d, bytes_accessed=4 * (f + rows) * d + 2 * rows * f, transcendentals=0
        ),
        name="terms",
    )(own, other, w_own, w_other)


def weight_kernel(idx_ref, act0_ref, act1_ref, act2_ref, act3_ref, own_ref, other_ref, out_ref, token_ref, grad_ref):
    @pl.when(pl.program_id(0) == 0)
    def _():
        for n in range(16):
            source = own_ref if n < 8 else other_ref
            rows = pl.ds(pl.multiple_of(idx_ref[n] * TB, TB), TB)
            grad_ref[rows, :] = source[n % 8 * TB : (n % 8 + 1) * TB, :]

    dims = (((0,), (0,)), ((), ()))
    quarter = act0_ref.shape[0]
    acc = None
    for n, act_ref in enumerate((act0_ref, act1_ref, act2_ref, act3_ref)):
        rows = slice(n * quarter, (n + 1) * quarter)
        term = lax.dot_general(act_ref[...], grad_ref[rows, :], dims, preferred_element_type=jnp.float32)
        acc = term if acc is None else acc + term
    out_ref[...] = acc
    token_ref[...] = jnp.zeros_like(token_ref)


def weight_product(index, acts, own, other):
    quarter, f = acts[0].shape
    d = own.shape[1]
    tile = 256
    act_spec = pl.BlockSpec((quarter, tile), lambda i: (0, i))
    return pl.pallas_call(
        weight_kernel,
        out_shape=(jax.ShapeDtypeStruct((f, d), jnp.float32), jax.ShapeDtypeStruct((8, 128), jnp.float32)),
        grid=(f // tile,),
        in_specs=[pl.BlockSpec(memory_space=pltpu.SMEM)] + [act_spec] * 4 + [WHOLE, WHOLE],
        out_specs=(pl.BlockSpec((tile, d), lambda i: (i, 0)), pl.BlockSpec((8, 128), lambda i: (0, 0))),
        scratch_shapes=[pltpu.VMEM((4 * quarter, d), own.dtype)],
        compiler_params=pltpu.CompilerParams(vmem_limit_bytes=24 * MIB),
        cost_estimate=pl.CostEstimate(
            flops=8 * quarter * f * d, bytes_accessed=8 * quarter * f + 4 * f * d, transcendentals=0
        ),
        name="weight_grad",
    )(index, *acts, own, other)


def finish_kernel(slope_ref, own_ref, *refs):
    out_ref = refs[-1]
    total = own_ref[...]
    for ref in refs[:-2]:
        total = total + ref[...].astype(jnp.float32)
    out_ref[...] = (total * slope_ref[...]).astype(out_ref.dtype)


def finish(slope, own, received, after):
    rows, f = slope.shape
    return pl.pallas_call(
        finish_kernel,
        out_shape=jax.ShapeDtypeStruct((rows, f), jnp.bfloat16),
        in_specs=[WHOLE] * (2 + len(received)) + [pl.BlockSpec(memory_space=pl.ANY)],
        out_specs=WHOLE,
        compiler_params=pltpu.CompilerParams(vmem_limit_bytes=8 * MIB),
        name="pre_grad",
    )(slope, own, *received, after)


def token_places():
    sizes = [SIZES[a] for a in AXES]
    places, tokens = np.zeros(sizes + [16], np.int32), np.zeros(sizes + [16], np.int32)
    for x, zl, core, zh, y in np.ndindex(*sizes):
        arrival = [(d, e) for d in range(4) for e in range(4)]
        for n, (d, e) in enumerate(arrival):
            yy, zz = (y + d) % 4, (zh + e) % 4
            place = (yy + core) % 2 * 8 + STEPS.index(((zz - x) % 4, (yy // 2 + zl) % 2))
            places[x, zl, core, zh, y, n] = place
            tokens[x, zl, core, zh, y, place] = (yy + core) % 2 * 8 + (yy // 2 + zl) % 2 * 4 + zz
    return np.concatenate([places.reshape(-1, 16), tokens.reshape(-1, 16)], axis=1)


def shards(pre_act, out_grad, down_weight):
    f, d_model = down_weight.shape
    tables = jnp.asarray(token_places())[lax.axis_index(AXES)]

    act = elementwise(gelu_kernel, pre_act, jnp.bfloat16, "gelu", 4)

    along_z = {e: fetch(out_grad, "zh", e) for e in (2, 1, 3)}
    act_x = gather_x(act)
    along_z, act_x = lax.optimization_barrier((along_z, act_x))
    along_z = jnp.concatenate([out_grad, along_z[1], along_z[2], along_z[3]], axis=0)
    far = {d: fetch(along_z, "y", d) for d in (2, 1, 3)}
    act_z = fetch(act_x, "zl", 1)
    act_x_other = fetch(act_x, "core", 1)

    down_weight, act_x_other = lax.optimization_barrier((down_weight, act_x_other))
    w_other = fetch(down_weight, "core", 1)
    grad_own, grad_other = order(tables[:16], [along_z, far[1], far[2], far[3]])
    grad_swapped = fetch(grad_other, "core", 1)
    act_z_other = fetch(act_z, "core", 1)

    part = terms(grad_own, grad_swapped, down_weight, w_other)
    part, act_z_other = lax.optimization_barrier((part, act_z_other))
    part = dict(zip(STEPS, part))
    beside = send_xz(part[2, 1], 0, 1)
    received = [send_xz(part[k], *k) for k in ((1, 0), (3, 0), (1, 1), (3, 1))]
    both = (part[2, 0] + beside.astype(jnp.float32)).astype(jnp.bfloat16)
    received.append(send_xz(both, 2, 0))
    part[0, 1], both = lax.optimization_barrier((part[0, 1], both))
    received.append(send_xz(part[0, 1], 0, 1))

    slope = elementwise(slope_kernel, pre_act, jnp.float32, "slope")
    tables, slope, both = lax.optimization_barrier((tables, slope, both))
    weight_grad, done = weight_product(tables[16:], (act_x, act_z, act_x_other, act_z_other), grad_own, grad_other)
    pre_grad = finish(slope, part[0, 0], received, done)
    return (pre_grad, weight_grad)


def solution(mesh):
    fine = Mesh(mesh.devices.reshape(tuple(SIZES[a] for a in AXES)), AXES)
    row, col = ("x", "zl", "core"), ("zh", "y")
    return jax.shard_map(
        shards,
        mesh=fine,
        in_specs=(P(row, col), P(col, row), P(col, row)),
        out_specs=(P(row, col), P(col, row)),
        check_vma=False,
    )
```

```python
import jax
import jax.numpy as jnp
import numpy as np
from jax import lax
from jax.experimental import pallas as pl
from jax.experimental.pallas import tpu as pltpu
from jax.sharding import Mesh, PartitionSpec as P

coeff_k = 0.7978845608
coeff_c = 0.044715

AXES = ("x", "zl", "core", "zh", "y")
SIZES = {"x": 4, "zl": 2, "core": 2, "zh": 4, "y": 4}
TB = 128
MIB = 1024 * 1024
STEPS = ((2, 1), (1, 0), (3, 0), (1, 1), (3, 1), (2, 0), (0, 1), (0, 0))
KEPT = ((0, 0), (2, 0), (0, 1))
WHOLE = pl.BlockSpec(memory_space=pltpu.VMEM)


def in_vmem(value):
    return pltpu.with_memory_space_constraint(value, pltpu.VMEM)


def in_hbm(value):
    return pltpu.with_memory_space_constraint(value, pltpu.HBM)


def fetch(value, axis, ahead):
    n = SIZES[axis]
    return lax.ppermute(value, axis, [((i + ahead) % n, i) for i in range(n)])


def repeat_kernel(*refs):
    sources, (out_ref, sems) = refs[:-2], refs[-2:]
    copies = []
    for n in range(out_ref.shape[0]):
        for i, source in enumerate(sources):
            rows = pl.ds(i * TB, TB)
            copies.append(pltpu.make_async_copy(source, out_ref.at[n, rows], sems.at[len(copies)]))
    for copy in copies:
        copy.start()
    for copy in copies:
        copy.wait()


def gather(axis, *values):
    n, f = SIZES[axis], values[0].shape[1]
    copies = pl.pallas_call(
        repeat_kernel,
        out_shape=pltpu.HBM((n, len(values) * TB, f), values[0].dtype),
        in_specs=[WHOLE] * len(values),
        out_specs=pl.BlockSpec(memory_space=pl.ANY),
        scratch_shapes=[pltpu.SemaphoreType.DMA((n * len(values),))],
        compiler_params=pltpu.CompilerParams(vmem_limit_bytes=4 * MIB),
        name=f"repeat_{axis}",
    )(*values)
    return lax.all_to_all(copies, axis, 0, 0).reshape(n * len(values) * TB, f)


def send_xz(value, dx, dz):
    pairs = []
    for x in range(4):
        for z in range(2):
            pairs.append((x * 2 + z, (x + dx) % 4 * 2 + (z + dz) % 2))
    return lax.ppermute(value, ("x", "zl"), pairs)


def tanh_of(z):
    return jnp.tanh(coeff_k * (z + coeff_c * z * z * z))


def gelu_kernel(pre_ref, act_ref):
    z = pre_ref[...].astype(jnp.float32)
    act_ref[...] = (0.5 * z * (1.0 + tanh_of(z))).astype(act_ref.dtype)


def slope_kernel(pre_ref, slope_ref):
    z = pre_ref[...].astype(jnp.float32)
    t = tanh_of(z)
    slope_ref[...] = 0.5 * (1.0 + t) + 0.5 * z * (1.0 - t * t) * coeff_k * (1.0 + 3.0 * coeff_c * z * z)


def elementwise(kernel, pre_act, dtype, name):
    rows, f = pre_act.shape
    tile = 64
    spec = pl.BlockSpec((tile, f), lambda i: (i, 0))
    return pl.pallas_call(
        kernel,
        out_shape=jax.ShapeDtypeStruct((rows, f), dtype),
        grid=(rows // tile,),
        in_specs=[spec],
        out_specs=spec,
        compiler_params=pltpu.CompilerParams(vmem_limit_bytes=8 * MIB),
        name=name,
    )(pre_act)


def order_kernel(first, idx_ref, *refs):
    own_ref, other_ref, sems = refs[-3:]
    sources = refs[:-5] if first else refs[:-3]
    blocks = [source.at[pl.ds(b, TB)] for source in sources for b in range(0, source.shape[0], TB)]
    for n, block in enumerate(blocks):
        place = idx_ref[first + n]
        rows = pl.ds(pl.multiple_of(place % 8 * TB, TB), TB)

        @pl.when(place >= 8)
        def _():
            pltpu.make_async_copy(block, other_ref.at[rows], sems.at[n]).start()

        @pl.when(place < 8)
        def _():
            pltpu.make_async_copy(block, own_ref.at[rows], sems.at[n]).start()

    for n, block in enumerate(blocks):
        pltpu.make_async_copy(block, own_ref.at[pl.ds(0, TB)], sems.at[n]).wait()


def order(index, first, sources, into=()):
    width = sources[0].shape[1]
    n = sum(s.shape[0] // TB for s in sources)
    out = pltpu.HBM((8 * TB, width), sources[0].dtype)
    any_spec = pl.BlockSpec(memory_space=pl.ANY)
    return pl.pallas_call(
        lambda *refs: order_kernel(first, *refs),
        out_shape=(out, out),
        in_specs=[pl.BlockSpec(memory_space=pltpu.SMEM)] + [WHOLE] * len(sources) + [any_spec] * len(into),
        out_specs=(any_spec, any_spec),
        scratch_shapes=[pltpu.SemaphoreType.DMA((n,))],
        input_output_aliases={1 + len(sources) + i: i for i in range(len(into))},
        compiler_params=pltpu.CompilerParams(vmem_limit_bytes=8 * MIB),
        name=f"order_tokens_{first}",
    )(index, *sources, *into)


def terms_kernel(own_ref, other_ref, w_own_ref, w_other_ref, *out_refs):
    dims = (((1,), (1,)), ((), ()))
    for n in range(0, len(out_refs), 2):
        rows = slice(n * TB, (n + 2) * TB)
        acc = lax.dot_general(own_ref[rows, :], w_own_ref[...], dims, preferred_element_type=jnp.float32)
        acc += lax.dot_general(other_ref[rows, :], w_other_ref[...], dims, preferred_element_type=jnp.float32)
        out_refs[n][...] = acc[:TB].astype(out_refs[n].dtype)
        out_refs[n + 1][...] = acc[TB:].astype(out_refs[n + 1].dtype)


def terms(own, other, w_own, w_other):
    f, d = w_own.shape
    rows = own.shape[0]
    tile = 512
    grad_spec = pl.BlockSpec((rows, d), lambda i: (0, 0))
    w_spec = pl.BlockSpec((tile, d), lambda i: (i, 0))
    return pl.pallas_call(
        terms_kernel,
        out_shape=[pltpu.HBM((TB, f), jnp.float32 if k in KEPT else jnp.bfloat16) for k in STEPS],
        grid=(f // tile,),
        in_specs=[grad_spec, WHOLE, w_spec, w_spec],
        out_specs=[pl.BlockSpec((TB, tile), lambda i: (0, i))] * len(STEPS),
        compiler_params=pltpu.CompilerParams(vmem_limit_bytes=24 * MIB),
        cost_estimate=pl.CostEstimate(
            flops=4 * rows * f * d, bytes_accessed=4 * (f + rows) * d + 2 * rows * f, transcendentals=0
        ),
        name="terms",
    )(in_hbm(own), in_vmem(other), w_own, w_other)


def weight_kernel(idx_ref, act_own_ref, act_other_ref, own_ref, other_ref, out_ref, token_ref, grad_ref):
    @pl.when(pl.program_id(0) == 0)
    def _():
        for n in range(16):
            source = own_ref if n < 8 else other_ref
            rows = pl.ds(pl.multiple_of(idx_ref[n] * TB, TB), TB)
            grad_ref[rows, :] = source[n % 8 * TB : (n % 8 + 1) * TB, :]

    dims = (((0,), (0,)), ((), ()))
    half = act_own_ref.shape[0]
    acc = lax.dot_general(act_own_ref[...], grad_ref[:half, :], dims, preferred_element_type=jnp.float32)
    acc += lax.dot_general(act_other_ref[...], grad_ref[half:, :], dims, preferred_element_type=jnp.float32)
    out_ref[...] = acc
    token_ref[...] = jnp.zeros_like(token_ref)


def weight_product(index, acts, own, other):
    half, f = acts[0].shape
    d = own.shape[1]
    tile = 256
    act_spec = pl.BlockSpec((half, tile), lambda i: (0, i))
    return pl.pallas_call(
        weight_kernel,
        out_shape=(jax.ShapeDtypeStruct((f, d), jnp.float32), jax.ShapeDtypeStruct((8, 128), jnp.float32)),
        grid=(f // tile,),
        in_specs=[pl.BlockSpec(memory_space=pltpu.SMEM)] + [act_spec] * 2 + [WHOLE, WHOLE],
        out_specs=(pl.BlockSpec((tile, d), lambda i: (i, 0)), pl.BlockSpec((8, 128), lambda i: (0, 0))),
        scratch_shapes=[pltpu.VMEM((2 * half, d), own.dtype)],
        compiler_params=pltpu.CompilerParams(vmem_limit_bytes=24 * MIB),
        cost_estimate=pl.CostEstimate(
            flops=4 * half * f * d, bytes_accessed=4 * half * f + 4 * f * d, transcendentals=0
        ),
        name="weight_grad",
    )(index, *acts, own, other)


def finish_kernel(slope_ref, own_ref, *refs):
    out_ref = refs[-1]
    total = own_ref[...]
    for ref in refs[:-2]:
        total = total + ref[...].astype(jnp.float32)
    out_ref[...] = (total * slope_ref[...]).astype(out_ref.dtype)


def finish(slope, own, received, after):
    rows, f = slope.shape
    return pl.pallas_call(
        finish_kernel,
        out_shape=jax.ShapeDtypeStruct((rows, f), jnp.bfloat16),
        in_specs=[WHOLE] * (2 + len(received)) + [pl.BlockSpec(memory_space=pl.ANY)],
        out_specs=WHOLE,
        compiler_params=pltpu.CompilerParams(vmem_limit_bytes=8 * MIB),
        name="pre_grad",
    )(slope, own, *received, after)


def token_places():
    sizes = [SIZES[a] for a in AXES]
    places, tokens = np.zeros(sizes + [16], np.int32), np.zeros(sizes + [16], np.int32)
    for x, zl, core, zh, y in np.ndindex(*sizes):
        arrival = [(d - y, 0) for d in range(4)] + [(d, e) for d in (0, 3, 1, 2) for e in (1, 2, 3)]
        for n, (d, e) in enumerate(arrival):
            yy, zz = (y + d) % 4, (zh + e) % 4
            place = (yy + core) % 2 * 8 + STEPS.index(((zz - x) % 4, (yy // 2 + zl) % 2))
            places[x, zl, core, zh, y, n] = place
            tokens[x, zl, core, zh, y, place] = (yy + core) % 2 * 8 + zz * 2 + (yy // 2 + zl) % 2
    return np.concatenate([places.reshape(-1, 16), tokens.reshape(-1, 16)], axis=1)


def shards(pre_act, out_grad, down_weight):
    f, d_model = down_weight.shape
    tables = jnp.asarray(token_places())[lax.axis_index(AXES)]

    along_z = {e: fetch(out_grad, "zh", e) for e in (2, 1, 3)}
    near = gather("y", out_grad)
    down_weight, along_z = lax.optimization_barrier((down_weight, along_z))
    along_z = jnp.concatenate([along_z[1], along_z[2], along_z[3]], axis=0)
    far = {d: fetch(along_z, "y", d) for d in (2, 1, 3)}
    act = elementwise(gelu_kernel, pre_act, jnp.bfloat16, "gelu")
    act_own = gather("x", act, fetch(act, "zl", 1))

    w_other = fetch(down_weight, "core", 1)
    grads = order(tables[:16], 0, [near, along_z])
    grads = order(tables[:16], 7, [far[3]], grads)
    grad_own, grad_other = order(tables[:16], 10, [far[1], far[2]], grads)
    grad_swapped = fetch(grad_other, "core", 1)

    part = terms(grad_own, grad_swapped, down_weight, w_other)
    part, act_own = lax.optimization_barrier((part, act_own))
    part = dict(zip(STEPS, part))
    beside = send_xz(part[2, 1], 0, 1)
    behind = send_xz(part[3, 1], 3, 0)
    received = [send_xz(part[k], *k) for k in ((1, 0), (3, 0), (1, 1))]
    beside, behind = lax.optimization_barrier((beside, behind))
    both = (part[2, 0] + beside.astype(jnp.float32)).astype(jnp.bfloat16)
    received.append(send_xz(both, 2, 0))
    received.append(send_xz((part[0, 1] + behind.astype(jnp.float32)).astype(jnp.bfloat16), 0, 1))
    act_other = fetch(act_own, "core", 1)

    slope = elementwise(slope_kernel, pre_act, jnp.float32, "slope")
    tables, slope = lax.optimization_barrier((tables, slope))
    weight_grad, done = weight_product(tables[16:], (act_own, act_other), grad_own, grad_other)
    pre_grad = finish(slope, part[0, 0], received, done)
    return (pre_grad, weight_grad)


def solution(mesh):
    fine = Mesh(mesh.devices.reshape(tuple(SIZES[a] for a in AXES)), AXES)
    row, col = ("x", "zl", "core"), ("zh", "y")
    return jax.shard_map(
        shards,
        mesh=fine,
        in_specs=(P(row, col), P(col, row), P(col, row)),
        out_specs=(P(row, col), P(col, row)),
        check_vma=False,
    )
```

```python
import jax
import jax.numpy as jnp
import numpy as np
from jax import lax
from jax.experimental import pallas as pl
from jax.experimental.pallas import tpu as pltpu
from jax.sharding import Mesh, PartitionSpec as P

coeff_k = 0.7978845608
coeff_c = 0.044715

AXES = ("x", "zl", "core", "zh", "y")
SIZES = {"x": 4, "zl": 2, "core": 2, "zh": 4, "y": 4}
TB = 128
MIB = 1024 * 1024
STEPS = ((2, 1), (1, 0), (3, 0), (1, 1), (3, 1), (2, 0), (0, 1), (0, 0))
KEPT = ((0, 0), (2, 0), (0, 1))
WHOLE = pl.BlockSpec(memory_space=pltpu.VMEM)


def in_vmem(value):
    return pltpu.with_memory_space_constraint(value, pltpu.VMEM)


def in_hbm(value):
    return pltpu.with_memory_space_constraint(value, pltpu.HBM)


def fetch(value, axis, ahead):
    n = SIZES[axis]
    return lax.ppermute(value, axis, [((i + ahead) % n, i) for i in range(n)])


def repeat_kernel(*refs):
    sources, (out_ref, sems) = refs[:-2], refs[-2:]
    copies = []
    for n in range(out_ref.shape[0]):
        for i, source in enumerate(sources):
            rows = pl.ds(i * TB, TB)
            copies.append(pltpu.make_async_copy(source, out_ref.at[n, rows], sems.at[len(copies)]))
    for copy in copies:
        copy.start()
    for copy in copies:
        copy.wait()


def gather(axis, *values):
    n, f = SIZES[axis], values[0].shape[1]
    copies = pl.pallas_call(
        repeat_kernel,
        out_shape=pltpu.HBM((n, len(values) * TB, f), values[0].dtype),
        in_specs=[WHOLE] * len(values),
        out_specs=pl.BlockSpec(memory_space=pl.ANY),
        scratch_shapes=[pltpu.SemaphoreType.DMA((n * len(values),))],
        compiler_params=pltpu.CompilerParams(vmem_limit_bytes=4 * MIB),
        name=f"repeat_{axis}",
    )(*values)
    return lax.all_to_all(copies, axis, 0, 0).reshape(n * len(values) * TB, f)


def send_xz(value, dx, dz):
    pairs = []
    for x in range(4):
        for z in range(2):
            pairs.append((x * 2 + z, (x + dx) % 4 * 2 + (z + dz) % 2))
    return lax.ppermute(value, ("x", "zl"), pairs)


def tanh_of(z):
    return jnp.tanh(coeff_k * (z + coeff_c * z * z * z))


def gelu_kernel(pre_ref, act_ref):
    z = pre_ref[...].astype(jnp.float32)
    act_ref[...] = (0.5 * z * (1.0 + tanh_of(z))).astype(act_ref.dtype)


def slope_kernel(pre_ref, slope_ref):
    z = pre_ref[...].astype(jnp.float32)
    t = tanh_of(z)
    slope_ref[...] = 0.5 * (1.0 + t) + 0.5 * z * (1.0 - t * t) * coeff_k * (1.0 + 3.0 * coeff_c * z * z)


def elementwise(kernel, pre_act, dtype, name):
    rows, f = pre_act.shape
    tile = 64
    spec = pl.BlockSpec((tile, f), lambda i: (i, 0))
    return pl.pallas_call(
        kernel,
        out_shape=jax.ShapeDtypeStruct((rows, f), dtype),
        grid=(rows // tile,),
        in_specs=[spec],
        out_specs=spec,
        compiler_params=pltpu.CompilerParams(vmem_limit_bytes=8 * MIB),
        name=name,
    )(pre_act)


def order_kernel(first, idx_ref, *refs):
    own_ref, other_ref, sems = refs[-3:]
    sources = refs[:-5] if first else refs[:-3]
    blocks = [source.at[pl.ds(b, TB)] for source in sources for b in range(0, source.shape[0], TB)]
    for n, block in enumerate(blocks):
        place = idx_ref[first + n]
        rows = pl.ds(pl.multiple_of(place % 8 * TB, TB), TB)

        @pl.when(place >= 8)
        def _():
            pltpu.make_async_copy(block, other_ref.at[rows], sems.at[n]).start()

        @pl.when(place < 8)
        def _():
            pltpu.make_async_copy(block, own_ref.at[rows], sems.at[n]).start()

    for n, block in enumerate(blocks):
        pltpu.make_async_copy(block, own_ref.at[pl.ds(0, TB)], sems.at[n]).wait()


def order(index, first, sources, into=()):
    width = sources[0].shape[1]
    n = sum(s.shape[0] // TB for s in sources)
    out = pltpu.HBM((8 * TB, width), sources[0].dtype)
    any_spec = pl.BlockSpec(memory_space=pl.ANY)
    return pl.pallas_call(
        lambda *refs: order_kernel(first, *refs),
        out_shape=(out, out),
        in_specs=[pl.BlockSpec(memory_space=pltpu.SMEM)] + [WHOLE] * len(sources) + [any_spec] * len(into),
        out_specs=(any_spec, any_spec),
        scratch_shapes=[pltpu.SemaphoreType.DMA((n,))],
        input_output_aliases={1 + len(sources) + i: i for i in range(len(into))},
        compiler_params=pltpu.CompilerParams(vmem_limit_bytes=8 * MIB),
        name=f"order_tokens_{first}",
    )(index, *sources, *into)


def terms_kernel(own_ref, other_ref, w_own_ref, w_other_ref, *out_refs):
    dims = (((1,), (1,)), ((), ()))
    for n in range(0, len(out_refs), 2):
        rows = slice(n * TB, (n + 2) * TB)
        acc = lax.dot_general(own_ref[rows, :], w_own_ref[...], dims, preferred_element_type=jnp.float32)
        acc += lax.dot_general(other_ref[rows, :], w_other_ref[...], dims, preferred_element_type=jnp.float32)
        out_refs[n][...] = acc[:TB].astype(out_refs[n].dtype)
        out_refs[n + 1][...] = acc[TB:].astype(out_refs[n + 1].dtype)


def terms(own, other, w_own, w_other):
    f, d = w_own.shape
    rows = own.shape[0]
    tile = 512
    grad_spec = pl.BlockSpec((rows, d), lambda i: (0, 0))
    w_spec = pl.BlockSpec((tile, d), lambda i: (i, 0))
    return pl.pallas_call(
        terms_kernel,
        out_shape=[pltpu.HBM((TB, f), jnp.float32 if k in KEPT else jnp.bfloat16) for k in STEPS],
        grid=(f // tile,),
        in_specs=[grad_spec, WHOLE, w_spec, w_spec],
        out_specs=[pl.BlockSpec((TB, tile), lambda i: (0, i))] * len(STEPS),
        compiler_params=pltpu.CompilerParams(vmem_limit_bytes=24 * MIB),
        cost_estimate=pl.CostEstimate(flops=MIB, bytes_accessed=MIB, transcendentals=0),
        name="terms",
    )(in_hbm(own), in_vmem(other), w_own, w_other)


def weight_kernel(idx_ref, act_own_ref, act_other_ref, own_ref, other_ref, out_ref, token_ref, grad_ref):
    @pl.when(pl.program_id(0) == 0)
    def _():
        for n in range(16):
            source = own_ref if n < 8 else other_ref
            rows = pl.ds(pl.multiple_of(idx_ref[n] * TB, TB), TB)
            grad_ref[rows, :] = source[n % 8 * TB : (n % 8 + 1) * TB, :]

    dims = (((0,), (0,)), ((), ()))
    half = act_own_ref.shape[0]
    acc = lax.dot_general(act_own_ref[...], grad_ref[:half, :], dims, preferred_element_type=jnp.float32)
    acc += lax.dot_general(act_other_ref[...], grad_ref[half:, :], dims, preferred_element_type=jnp.float32)
    out_ref[...] = acc
    token_ref[...] = jnp.zeros_like(token_ref)


def weight_product(index, acts, own, other):
    half, f = acts[0].shape
    d = own.shape[1]
    tile = 256
    act_spec = pl.BlockSpec((half, tile), lambda i: (0, i))
    return pl.pallas_call(
        weight_kernel,
        out_shape=(jax.ShapeDtypeStruct((f, d), jnp.float32), jax.ShapeDtypeStruct((8, 128), jnp.float32)),
        grid=(f // tile,),
        in_specs=[pl.BlockSpec(memory_space=pltpu.SMEM)] + [act_spec] * 2 + [WHOLE, WHOLE],
        out_specs=(pl.BlockSpec((tile, d), lambda i: (i, 0)), pl.BlockSpec((8, 128), lambda i: (0, 0))),
        scratch_shapes=[pltpu.VMEM((2 * half, d), own.dtype)],
        compiler_params=pltpu.CompilerParams(vmem_limit_bytes=24 * MIB),
        cost_estimate=pl.CostEstimate(
            flops=4 * half * f * d, bytes_accessed=4 * half * f + 4 * f * d, transcendentals=0
        ),
        name="weight_grad",
    )(index, *acts, own, other)


def merge_kernel(kept_ref, received_ref, out_ref):
    out_ref[...] = (kept_ref[...] + received_ref[...].astype(jnp.float32)).astype(out_ref.dtype)


def merge(kept, received):
    return pl.pallas_call(
        merge_kernel,
        out_shape=jax.ShapeDtypeStruct(received.shape, received.dtype),
        in_specs=[WHOLE, WHOLE],
        out_specs=WHOLE,
        compiler_params=pltpu.CompilerParams(vmem_limit_bytes=8 * MIB),
        cost_estimate=pl.CostEstimate(flops=30_000_000_000, bytes_accessed=MIB, transcendentals=0),
        name="merge",
    )(in_hbm(kept), received)


def finish_kernel(slope_ref, own_ref, *refs):
    out_ref = refs[-1]
    total = own_ref[...]
    for ref in refs[:-2]:
        total = total + ref[...].astype(jnp.float32)
    out_ref[...] = (total * slope_ref[...]).astype(out_ref.dtype)


def finish(slope, own, received, after):
    rows, f = slope.shape
    return pl.pallas_call(
        finish_kernel,
        out_shape=jax.ShapeDtypeStruct((rows, f), jnp.bfloat16),
        in_specs=[WHOLE] * (2 + len(received)) + [pl.BlockSpec(memory_space=pl.ANY)],
        out_specs=WHOLE,
        compiler_params=pltpu.CompilerParams(vmem_limit_bytes=8 * MIB),
        name="pre_grad",
    )(in_hbm(slope), in_hbm(own), *received, after)


def token_places():
    sizes = [SIZES[a] for a in AXES]
    places, tokens = np.zeros(sizes + [16], np.int32), np.zeros(sizes + [16], np.int32)
    for x, zl, core, zh, y in np.ndindex(*sizes):
        arrival = [(d - y, 0) for d in range(4)] + [(d, e) for d in (0, 3, 1, 2) for e in (1, 2, 3)]
        for n, (d, e) in enumerate(arrival):
            yy, zz = (y + d) % 4, (zh + e) % 4
            place = (yy + core) % 2 * 8 + STEPS.index(((zz - x) % 4, (yy // 2 + zl) % 2))
            places[x, zl, core, zh, y, n] = place
            tokens[x, zl, core, zh, y, place] = (yy + core) % 2 * 8 + zz * 2 + (yy // 2 + zl) % 2
    return np.concatenate([places.reshape(-1, 16), tokens.reshape(-1, 16)], axis=1)


def shards(pre_act, out_grad, down_weight):
    f, d_model = down_weight.shape
    tables = jnp.asarray(token_places())[lax.axis_index(AXES)]

    along_z = {e: fetch(out_grad, "zh", e) for e in (2, 1, 3)}
    near = gather("y", out_grad)
    down_weight, along_z = lax.optimization_barrier((down_weight, along_z))
    along_z = jnp.concatenate([along_z[1], along_z[2], along_z[3]], axis=0)
    far = {d: fetch(along_z, "y", d) for d in (2, 1, 3)}
    act = elementwise(gelu_kernel, pre_act, jnp.bfloat16, "gelu")
    act_own = gather("x", act, fetch(act, "zl", 1))

    w_other = fetch(down_weight, "core", 1)
    slope = elementwise(slope_kernel, pre_act, jnp.float32, "slope")
    tables, slope = lax.optimization_barrier((tables, slope))
    grads = order(tables[:16], 0, [near, along_z])
    grads = order(tables[:16], 7, [far[3]], grads)
    grad_own, grad_other = order(tables[:16], 10, [far[1], far[2]], grads)
    grad_swapped = fetch(grad_other, "core", 1)

    part = terms(grad_own, grad_swapped, down_weight, w_other)
    part = dict(zip(STEPS, part))
    beside = send_xz(part[2, 1], 0, 1)
    behind = send_xz(part[3, 1], 3, 0)
    received = [send_xz(part[k], *k) for k in ((1, 0), (3, 0), (1, 1))]
    both = merge(part[2, 0], beside)
    received.append(send_xz(both, 2, 0))
    behind, both = lax.optimization_barrier((behind, both))
    received.append(send_xz((part[0, 1] + behind.astype(jnp.float32)).astype(jnp.bfloat16), 0, 1))
    act_other = fetch(act_own, "core", 1)

    weight_grad, done = weight_product(tables[16:], (act_own, act_other), grad_own, grad_other)
    pre_grad = finish(slope, part[0, 0], received, done)
    return (pre_grad, weight_grad)


def solution(mesh):
    fine = Mesh(mesh.devices.reshape(tuple(SIZES[a] for a in AXES)), AXES)
    row, col = ("x", "zl", "core"), ("zh", "y")
    return jax.shard_map(
        shards,
        mesh=fine,
        in_specs=(P(row, col), P(col, row), P(col, row)),
        out_specs=(P(row, col), P(col, row)),
        check_vma=False,
    )
```

```python
import jax
import jax.numpy as jnp
import numpy as np
from jax import lax
from jax.experimental import pallas as pl
from jax.experimental.pallas import tpu as pltpu
from jax.sharding import Mesh, PartitionSpec as P

coeff_k = 0.7978845608
coeff_c = 0.044715

AXES = ("x", "zl", "core", "zh", "y")
SIZES = {"x": 4, "zl": 2, "core": 2, "zh": 4, "y": 4}
TB = 128
MIB = 1024 * 1024
STEPS = ((2, 1), (1, 0), (3, 0), (1, 1), (3, 1), (2, 0), (0, 1), (0, 0))
KEPT = ((0, 0), (2, 0), (0, 1))
WHOLE = pl.BlockSpec(memory_space=pltpu.VMEM)


def in_vmem(value):
    return pltpu.with_memory_space_constraint(value, pltpu.VMEM)


def in_hbm(value):
    return pltpu.with_memory_space_constraint(value, pltpu.HBM)


def fetch(value, axis, ahead):
    n = SIZES[axis]
    return lax.ppermute(value, axis, [((i + ahead) % n, i) for i in range(n)])


def repeat_kernel(*refs):
    sources, (out_ref, sems) = refs[:-2], refs[-2:]
    copies = []
    for n in range(out_ref.shape[0]):
        for i, source in enumerate(sources):
            rows = pl.ds(i * TB, TB)
            copies.append(pltpu.make_async_copy(source, out_ref.at[n, rows], sems.at[len(copies)]))
    for copy in copies:
        copy.start()
    for copy in copies:
        copy.wait()


def gather(axis, *values):
    n, f = SIZES[axis], values[0].shape[1]
    copies = pl.pallas_call(
        repeat_kernel,
        out_shape=pltpu.HBM((n, len(values) * TB, f), values[0].dtype),
        in_specs=[WHOLE] * len(values),
        out_specs=pl.BlockSpec(memory_space=pl.ANY),
        scratch_shapes=[pltpu.SemaphoreType.DMA((n * len(values),))],
        compiler_params=pltpu.CompilerParams(vmem_limit_bytes=4 * MIB),
        name=f"repeat_{axis}",
    )(*values)
    return lax.all_to_all(copies, axis, 0, 0).reshape(n * len(values) * TB, f)


def send_xz(value, dx, dz):
    pairs = []
    for x in range(4):
        for z in range(2):
            pairs.append((x * 2 + z, (x + dx) % 4 * 2 + (z + dz) % 2))
    return lax.ppermute(value, ("x", "zl"), pairs)


def tanh_of(z):
    return jnp.tanh(coeff_k * (z + coeff_c * z * z * z))


def gelu_kernel(pre_ref, act_ref):
    z = pre_ref[...].astype(jnp.float32)
    act_ref[...] = (0.5 * z * (1.0 + tanh_of(z))).astype(act_ref.dtype)


def slope_kernel(pre_ref, slope_ref):
    z = pre_ref[...].astype(jnp.float32)
    t = tanh_of(z)
    slope_ref[...] = 0.5 * (1.0 + t) + 0.5 * z * (1.0 - t * t) * coeff_k * (1.0 + 3.0 * coeff_c * z * z)


def elementwise(kernel, pre_act, dtype, name):
    rows, f = pre_act.shape
    tile = 64
    spec = pl.BlockSpec((tile, f), lambda i: (i, 0))
    return pl.pallas_call(
        kernel,
        out_shape=jax.ShapeDtypeStruct((rows, f), dtype),
        grid=(rows // tile,),
        in_specs=[spec],
        out_specs=spec,
        compiler_params=pltpu.CompilerParams(vmem_limit_bytes=8 * MIB),
        name=name,
    )(pre_act)


def order_kernel(first, idx_ref, *refs):
    own_ref, other_ref, sems = refs[-3:]
    sources = refs[:-5] if first else refs[:-3]
    blocks = [source.at[pl.ds(b, TB)] for source in sources for b in range(0, source.shape[0], TB)]
    for n, block in enumerate(blocks):
        place = idx_ref[first + n]
        rows = pl.ds(pl.multiple_of(place % 8 * TB, TB), TB)

        @pl.when(place >= 8)
        def _():
            pltpu.make_async_copy(block, other_ref.at[rows], sems.at[n]).start()

        @pl.when(place < 8)
        def _():
            pltpu.make_async_copy(block, own_ref.at[rows], sems.at[n]).start()

    for n, block in enumerate(blocks):
        pltpu.make_async_copy(block, own_ref.at[pl.ds(0, TB)], sems.at[n]).wait()


def order(index, first, sources, into=()):
    width = sources[0].shape[1]
    n = sum(s.shape[0] // TB for s in sources)
    out = pltpu.HBM((8 * TB, width), sources[0].dtype)
    any_spec = pl.BlockSpec(memory_space=pl.ANY)
    return pl.pallas_call(
        lambda *refs: order_kernel(first, *refs),
        out_shape=(out, out),
        in_specs=[pl.BlockSpec(memory_space=pltpu.SMEM)] + [WHOLE] * len(sources) + [any_spec] * len(into),
        out_specs=(any_spec, any_spec),
        scratch_shapes=[pltpu.SemaphoreType.DMA((n,))],
        input_output_aliases={1 + len(sources) + i: i for i in range(len(into))},
        compiler_params=pltpu.CompilerParams(vmem_limit_bytes=8 * MIB),
        name=f"order_tokens_{first}",
    )(index, *sources, *into)


def terms_kernel(own_ref, other_ref, w_own_ref, w_other_ref, *out_refs):
    dims = (((1,), (1,)), ((), ()))
    for n in range(0, len(out_refs), 2):
        rows = slice(n * TB, (n + 2) * TB)
        acc = lax.dot_general(own_ref[rows, :], w_own_ref[...], dims, preferred_element_type=jnp.float32)
        acc += lax.dot_general(other_ref[rows, :], w_other_ref[...], dims, preferred_element_type=jnp.float32)
        out_refs[n][...] = acc[:TB].astype(out_refs[n].dtype)
        out_refs[n + 1][...] = acc[TB:].astype(out_refs[n + 1].dtype)


def terms(own, other, w_own, w_other):
    f, d = w_own.shape
    rows = own.shape[0]
    tile = 512
    grad_spec = pl.BlockSpec((rows, d), lambda i: (0, 0))
    w_spec = pl.BlockSpec((tile, d), lambda i: (i, 0))
    return pl.pallas_call(
        terms_kernel,
        out_shape=[pltpu.HBM((TB, f), jnp.float32 if k in KEPT else jnp.bfloat16) for k in STEPS],
        grid=(f // tile,),
        in_specs=[grad_spec, WHOLE, w_spec, w_spec],
        out_specs=[pl.BlockSpec((TB, tile), lambda i: (0, i))] * len(STEPS),
        compiler_params=pltpu.CompilerParams(vmem_limit_bytes=24 * MIB),
        cost_estimate=pl.CostEstimate(flops=MIB, bytes_accessed=MIB, transcendentals=0),
        name="terms",
    )(in_hbm(own), in_vmem(other), w_own, w_other)


def weight_kernel(idx_ref, act_own_ref, act_other_ref, own_ref, other_ref, out_ref, token_ref, grad_ref):
    @pl.when(pl.program_id(0) == 0)
    def _():
        for n in range(16):
            source = own_ref if n < 8 else other_ref
            rows = pl.ds(pl.multiple_of(idx_ref[n] * TB, TB), TB)
            grad_ref[rows, :] = source[n % 8 * TB : (n % 8 + 1) * TB, :]

    dims = (((0,), (0,)), ((), ()))
    half = act_own_ref.shape[0]
    acc = lax.dot_general(act_own_ref[...], grad_ref[:half, :], dims, preferred_element_type=jnp.float32)
    acc += lax.dot_general(act_other_ref[...], grad_ref[half:, :], dims, preferred_element_type=jnp.float32)
    out_ref[...] = acc
    token_ref[...] = jnp.zeros_like(token_ref)


def weight_product(index, acts, own, other):
    half, f = acts[0].shape
    d = own.shape[1]
    tile = 256
    act_spec = pl.BlockSpec((half, tile), lambda i: (0, i))
    return pl.pallas_call(
        weight_kernel,
        out_shape=(jax.ShapeDtypeStruct((f, d), jnp.float32), jax.ShapeDtypeStruct((8, 128), jnp.float32)),
        grid=(f // tile,),
        in_specs=[pl.BlockSpec(memory_space=pltpu.SMEM)] + [act_spec] * 2 + [WHOLE, WHOLE],
        out_specs=(pl.BlockSpec((tile, d), lambda i: (i, 0)), pl.BlockSpec((8, 128), lambda i: (0, 0))),
        scratch_shapes=[pltpu.VMEM((2 * half, d), own.dtype)],
        compiler_params=pltpu.CompilerParams(vmem_limit_bytes=24 * MIB),
        cost_estimate=pl.CostEstimate(
            flops=4 * half * f * d, bytes_accessed=4 * half * f + 4 * f * d, transcendentals=0
        ),
        name="weight_grad",
    )(index, *acts, own, other)


def merge_kernel(kept_ref, received_ref, out_ref):
    out_ref[...] = (kept_ref[...] + received_ref[...].astype(jnp.float32)).astype(out_ref.dtype)


def merge(kept, received):
    return pl.pallas_call(
        merge_kernel,
        out_shape=jax.ShapeDtypeStruct(received.shape, received.dtype),
        in_specs=[WHOLE, WHOLE],
        out_specs=WHOLE,
        compiler_params=pltpu.CompilerParams(vmem_limit_bytes=8 * MIB),
        cost_estimate=pl.CostEstimate(flops=30_000_000_000, bytes_accessed=MIB, transcendentals=0),
        name="merge",
    )(in_hbm(kept), received)


def finish_kernel(slope_ref, own_ref, *refs):
    out_ref = refs[-1]
    total = own_ref[...]
    for ref in refs[:-2]:
        total = total + ref[...].astype(jnp.float32)
    out_ref[...] = (total * slope_ref[...]).astype(out_ref.dtype)


def finish(slope, own, received, after):
    rows, f = slope.shape
    return pl.pallas_call(
        finish_kernel,
        out_shape=jax.ShapeDtypeStruct((rows, f), jnp.bfloat16),
        in_specs=[WHOLE] * (2 + len(received)) + [pl.BlockSpec(memory_space=pl.ANY)],
        out_specs=WHOLE,
        compiler_params=pltpu.CompilerParams(vmem_limit_bytes=8 * MIB),
        name="pre_grad",
    )(slope, own, *received, after)


def token_places():
    sizes = [SIZES[a] for a in AXES]
    places, tokens = np.zeros(sizes + [16], np.int32), np.zeros(sizes + [16], np.int32)
    for x, zl, core, zh, y in np.ndindex(*sizes):
        arrival = [(d - y, 0) for d in range(4)] + [(d, e) for d in (0, 3, 1, 2) for e in (1, 2, 3)]
        for n, (d, e) in enumerate(arrival):
            yy, zz = (y + d) % 4, (zh + e) % 4
            place = (yy + core) % 2 * 8 + STEPS.index(((zz - x) % 4, (yy // 2 + zl) % 2))
            places[x, zl, core, zh, y, n] = place
            tokens[x, zl, core, zh, y, place] = (yy + core) % 2 * 8 + zz * 2 + (yy // 2 + zl) % 2
    return np.concatenate([places.reshape(-1, 16), tokens.reshape(-1, 16)], axis=1)


def shards(pre_act, out_grad, down_weight):
    f, d_model = down_weight.shape
    tables = jnp.asarray(token_places())[lax.axis_index(AXES)]

    along_z = {e: fetch(out_grad, "zh", e) for e in (2, 1, 3)}
    near = gather("y", out_grad)
    down_weight, along_z = lax.optimization_barrier((down_weight, along_z))
    along_z = jnp.concatenate([along_z[1], along_z[2], along_z[3]], axis=0)
    far = {d: fetch(along_z, "y", d) for d in (2, 1, 3)}
    act = elementwise(gelu_kernel, pre_act, jnp.bfloat16, "gelu")
    act_own = gather("x", act, fetch(act, "zl", 1))

    w_other = fetch(down_weight, "core", 1)
    slope = elementwise(slope_kernel, pre_act, jnp.float32, "slope")
    tables, slope = lax.optimization_barrier((tables, slope))
    grads = order(tables[:16], 0, [near, along_z])
    grads = order(tables[:16], 7, [far[3]], grads)
    grad_own, grad_other = order(tables[:16], 10, [far[1], far[2]], grads)
    grad_swapped = fetch(grad_other, "core", 1)

    part = terms(grad_own, grad_swapped, down_weight, w_other)
    part = dict(zip(STEPS, part))
    beside = send_xz(part[2, 1], 0, 1)
    behind = send_xz(part[3, 1], 3, 0)
    received = [send_xz(part[k], *k) for k in ((1, 0), (3, 0), (1, 1))]
    both = merge(part[2, 0], beside)
    received.append(send_xz(both, 2, 0))
    behind, both = lax.optimization_barrier((behind, both))
    received.append(send_xz((part[0, 1] + behind.astype(jnp.float32)).astype(jnp.bfloat16), 0, 1))
    act_other = fetch(act_own, "core", 1)

    weight_grad, done = weight_product(tables[16:], (act_own, act_other), grad_own, grad_other)
    pre_grad = finish(slope, part[0, 0], received, done)
    return (pre_grad, weight_grad)


def solution(mesh):
    fine = Mesh(mesh.devices.reshape(tuple(SIZES[a] for a in AXES)), AXES)
    row, col = ("x", "zl", "core"), ("zh", "y")
    return jax.shard_map(
        shards,
        mesh=fine,
        in_specs=(P(row, col), P(col, row), P(col, row)),
        out_specs=(P(row, col), P(col, row)),
        check_vma=False,
    )
```
